32 devices in a mesh: groups: 2 (over x), rows: 8 (over z, y), cls: 2 (over core).
Axes of the slice: x: 2, y: 2, z: 4, core: 2. Of those that a mesh axis runs over, the one named last changes fastest.
Arguments:
- embeddings: bfloat16 [8192, 1024], P(('groups', 'rows')), parts along dimension 0, may hold values from -6 to 6
- omega: bfloat16 [1024, 3072], replicated, may hold values from -0.25 to 0.25
- phases: float32 [3072], replicated, may hold values from -3.140625 to 3.140625
- index_list: int32 [3072], replicated, may hold values from 0 to 3071, each once
- inverse_store: bfloat16 [16, 1024, 1024], P(('groups', 'rows')), parts along dimension 0, as said below
- roots: int32 [3], replicated, may hold values from 0 to 7, as said below
- residual_in: bfloat16 [8192, 1024], P(('groups', 'rows'), 'cls'), parts along dimension 0, may hold values from -6 to 6
Outputs:
- changes: bfloat16 [6, 1024, 1024], P('groups', None, 'cls'), parts along dimension 0
- residual_out: bfloat16 [8192, 1024], P(('groups', 'rows'), 'cls'), parts along dimension 0
The draws below stay inside these ranges and needn't reach their ends.
There are 2 independent parts, one for each index of `groups`. The reference program is written for one: setup_inputs(seed, part) draws one part's arguments, and reference() takes and returns one part's arrays. A program takes and returns all parts, laid end to end along the dimension named above; an argument that names none is the same for every part. Nothing has to cross between parts.
Inputs may be any that keep to these rules, and one draw needn't show every extreme that they name: `roots`: entries are distinct; 0 and 7 are always among them. `inverse_store`: each slot is a dense matrix.
All inputs are finite; a program needn't handle non-finite values.
Results may differ from the reference program's by a relative error of at most 0.0051.
Values may be sent and summed in bfloat16 or wider, within the bound.
A program may use at most 64 MiB of HBM per device.

```python
import math
import jax
import jax.numpy as jnp
from jax import lax

DIN = 1024
F = 1024
C = 1024
NB = 3
ROWS_DEV = 512
TOKENS = 4096
POOL = 3072
N_ROWS = 8


def draw_inverse_store(key, part):
    first, second = jax.random.split(jax.random.fold_in(key, 17))
    shrink = F / (ROWS_DEV * N_ROWS)
    diag_part = jnp.exp(jax.random.uniform(first, (N_ROWS, F), jnp.float32, math.log(0.5), math.log(2.0)))
    noise = jax.random.normal(second, (N_ROWS, F, F), jnp.float32) * (0.6 / math.sqrt(F))
    eye_table = jnp.eye(F, dtype=jnp.float32)
    matrix = (noise + diag_part[:, :, None] * eye_table[None, :, :]) * shrink
    return matrix.astype(jnp.bfloat16)


def draw_roots(key, part):
    first, second = jax.random.split(jax.random.fold_in(key, 29))
    middle = jax.random.permutation(first, jnp.arange(1, N_ROWS - 1, dtype=jnp.int32))[:NB - 2]
    picked = jnp.concatenate([jnp.array([0, N_ROWS - 1], dtype=jnp.int32), middle.astype(jnp.int32)])
    return jax.random.permutation(second, picked).astype(jnp.int32)


def levels(stream_key, shape, cuts, smallest, largest):
    gain = 1.0
    for dim, parts in cuts:
        heights = jax.random.uniform(jax.random.fold_in(jax.random.fold_in(stream_key, 6), dim), (parts,), jnp.float32, smallest / len(cuts), largest / len(cuts))
        gain = gain * jnp.repeat(jnp.exp(heights), shape[dim] // parts).reshape((-1,) + (1,) * (len(shape) - 1 - dim))
    return gain


def normal_values(rng, dims, scale, limit, cuts=(), kind=jnp.bfloat16):
    values = jax.random.normal(rng, dims, jnp.float32) * scale
    if len(cuts) > 0:
        values = levels(rng, dims, cuts, -0.22, 0.18) * values
    return jnp.clip(values, min=-limit, max=limit).astype(kind)


def setup_inputs(seed: int = 0, part: int = 0) -> dict:
    splits = jax.random.split(jax.random.key(seed), 8)
    part_splits = jax.random.split(jax.random.fold_in(splits[7], part), 8)
    return {
        "embeddings": normal_values(part_splits[0], (TOKENS, DIN), 1.0, 6.0, ((0, 8),)),
        "omega": normal_values(splits[1], (DIN, POOL), (DIN // 2) ** -0.5, 0.25),
        "phases": jnp.clip(jax.random.uniform(splits[2], (POOL,), jnp.float32, -3.140625, 3.140625), -3.140625, 3.140625),
        "index_list": jax.random.permutation(splits[3], POOL).astype(jnp.int32),
        "inverse_store": draw_inverse_store(jax.random.fold_in(jax.random.fold_in(splits[7], part), 71), part),
        "roots": draw_roots(jax.random.fold_in(splits[7], 71), part),
        "residual_in": normal_values(part_splits[6], (TOKENS, C), 1.0, 6.0, ((0, 8), (1, 2))),
    }


def reference(embeddings, omega, phases, index_list, inverse_store, roots, residual_in):
    residual = residual_in.astype(jnp.float32)
    scale = math.sqrt(2.0 / F)
    results = []
    for block in range(NB):
        cols = index_list[block * F:(block + 1) * F]
        chosen = jnp.take(omega, cols, axis=1)
        proj = jnp.dot(embeddings, chosen, preferred_element_type=jnp.float32)
        feats = (scale * jnp.cos(proj + jnp.take(phases, cols)[None, :])).astype(jnp.bfloat16)
        rounded = residual.astype(jnp.bfloat16)
        corr = jnp.dot(feats.T, rounded, preferred_element_type=jnp.float32).astype(jnp.bfloat16)
        inverse = lax.dynamic_index_in_dim(inverse_store, roots[block].astype(jnp.int32), 0, keepdims=False)
        change = jnp.dot(inverse, corr, preferred_element_type=jnp.float32).astype(jnp.bfloat16)
        residual = residual - jnp.dot(feats, change, preferred_element_type=jnp.float32)
        results.append(change)
    return (jnp.stack(results), residual.astype(jnp.bfloat16))
```

```python
import functools
import math

import jax
import jax.numpy as jnp
import numpy as np
from jax import lax
from jax.experimental import pallas as pl
from jax.experimental.pallas import tpu as pltpu
from jax.sharding import PartitionSpec as P

MESH = pl.DeviceIdType.MESH
F32 = jnp.float32
BF16 = jnp.bfloat16


def cos_coefficients(degree):
    top = math.pi**2 * 1.0001
    cheb = np.polynomial.chebyshev.Chebyshev.interpolate(
        lambda u: np.cos(np.sqrt(np.maximum(u, 0.0))), degree, domain=[0.0, top]
    )
    return [float(c) for c in cheb.convert(kind=np.polynomial.Polynomial).coef]


COS = cos_coefficients(7)
TWO_PI_HI = 6.28125
TWO_PI_LO = 2.0 * math.pi - TWO_PI_HI


def cosine(x):
    turns = jnp.round(x * (1.0 / (2.0 * math.pi)))
    r = (x - turns * TWO_PI_HI) - turns * TWO_PI_LO
    u = r * r
    y = jnp.full_like(u, COS[-1])
    for c in COS[-2::-1]:
        y = y * u + c
    return y


def tile_of(size, want):
    return want if size % want == 0 else size


def body(
    n, inner, roots_ref, emb_ref, omega_ref, phases_ref, index_ref, slot_ref, res_in_ref,
    changes_ref, res_ref,
    plain, feats, resid, corr, ybuf, zout, zbuf, chg, abuf, inv,
    a_sem, ys_sem, zs_sem, cz_sem, cy_sem, iz_sem, iy_sem, ic_sem, loc_sem, out_sem,
):
    outer = n // inner
    me = lax.axis_index("rows")
    core = lax.axis_index("cls")
    mi = lax.rem(me, inner)
    mo = lax.div(me, inner)
    partner = mo * inner + (inner - 1 - mi)
    rows, din = emb_ref.shape
    pool = omega_ref.shape[1]
    blocks, width = chg.shape[0], chg.shape[3]
    classes = resid.shape[1]
    share = classes // n
    pending = []

    def send(src, dst, sems, device):
        copy = pltpu.make_async_remote_copy(
            src_ref=src, dst_ref=dst, send_sem=sems[0], recv_sem=sems[1],
            device_id=device, device_id_type=MESH,
        )
        copy.start()
        pending.append(copy)
        return copy

    def arrived(dst, sems):
        pltpu.make_async_remote_copy(
            src_ref=dst, dst_ref=dst, send_sem=sems[0], recv_sem=sems[1],
            device_id={"rows": partner}, device_id_type=MESH,
        ).wait_recv()

    def at(sem, *idx):
        return sem.at[(0, *idx)], sem.at[(1, *idx)]

    def other(d):
        return lax.rem(mo + d, outer)

    barrier = pltpu.get_barrier_semaphore()
    for d in range(1, n):
        pl.semaphore_signal(
            barrier, inc=1, device_id={"rows": lax.rem(me + d, n)}, device_id_type=MESH
        )
    pl.semaphore_signal(barrier, inc=1, device_id={"cls": 1 - core}, device_id_type=MESH)
    pl.semaphore_wait(barrier, n)

    for d in range(1, n):
        to = lax.rem(me + d, n)
        send(slot_ref.at[core, to], abuf.at[me], at(a_sem, d), {"rows": to})
    own = pltpu.make_async_copy(slot_ref.at[core, me], abuf.at[me], loc_sem.at[0])
    own.start()
    res_load = pltpu.make_async_copy(res_in_ref, res_ref, loc_sem.at[1])
    res_load.start()

    scale = math.sqrt(2.0 / width)
    wide = tile_of(pool, 512)

    @pl.loop(0, pool // wide)
    def _(t):
        cols = pl.ds(pl.multiple_of(t * wide, wide), wide)
        proj = jnp.dot(emb_ref[...], omega_ref[:, cols], preferred_element_type=F32)
        plain[:, cols] = (scale * cosine(proj + phases_ref[:, cols])).astype(BF16)

    narrow = tile_of(pool, 256)

    @pl.loop(0, pool // narrow)
    def _(t):
        cols = pl.ds(pl.multiple_of(t * narrow, narrow), narrow)
        line = lax.broadcasted_iota(jnp.int32, (pool, narrow), 0)
        pick = jnp.where(line == index_ref[:, cols], 1.0, 0.0).astype(BF16)
        feats[:, cols] = jnp.dot(plain[...], pick, preferred_element_type=F32).astype(BF16)

    res_load.wait()
    resid[...] = res_ref[...].astype(F32)

    step = tile_of(width, 256)

    def correlate(b):
        rounded = resid[...].astype(BF16)

        @pl.loop(0, width // step)
        def _(t):
            here = pl.multiple_of(t * step, step)
            part = lax.dot_general(
                rounded, feats[:, pl.ds(b * width + here, step)],
                (((0,), (0,)), ((), ())), preferred_element_type=F32,
            )
            corr[b, :, :, pl.ds(here, step)] = part.astype(BF16).reshape(n, share, step)

        for d in range(1, outer + 1):
            o = other(d)
            send(
                corr.at[b, o * inner + (inner - 1 - mi)], ybuf.at[b, o],
                at(ys_sem, b, d % outer), {"rows": partner},
            )

    def pair_sum(b, d):
        o = other(d)
        arrived(ybuf.at[b, o], at(ys_sem, b, d % outer))
        return corr[b, o * inner + mi].astype(F32) + ybuf[b, o].astype(F32)

    def scatter(b):
        for d in range(1, outer):
            o = other(d)
            zout[b, d] = pair_sum(b, d).astype(BF16)
            send(zout.at[b, d], zbuf.at[b, d], at(zs_sem, b, d), {"rows": o * inner + mi})

    def total(b):
        acc = pair_sum(b, 0)
        for d in range(1, outer):
            arrived(zbuf.at[b, d], at(zs_sem, b, d))
            acc = acc + zbuf[b, d].astype(F32)
        return acc.astype(BF16)

    def gather_first(ref, z_sem, y_sem, b):
        for d in range(1, outer):
            send(ref.at[me], ref.at[me], at(z_sem, b, d), {"rows": other(d) * inner + mi})
        send(ref.at[me], ref.at[me], at(y_sem, b, 0), {"rows": partner})

    def gather_second(ref, z_sem, y_sem, b):
        for d in range(1, outer):
            src = lax.rem(mo - d + outer, outer) * inner + mi
            arrived(ref.at[src], at(z_sem, b, d))
            send(ref.at[src], ref.at[src], at(y_sem, b, d), {"rows": partner})

    def gather_third(ref, y_sem, b):
        for d in range(outer):
            src = lax.rem(mo - d + outer, outer) * inner + (inner - 1 - mi)
            arrived(ref.at[src], at(y_sem, b, d))

    def inv_first(b):
        gather_first(inv.at[b, core], iz_sem, iy_sem, b)

    def inv_second(b):
        gather_second(inv.at[b, core], iz_sem, iy_sem, b)

    def inv_third(b):
        gather_third(inv.at[b, core], iy_sem, b)
        send(inv.at[b, core], inv.at[b, core], at(ic_sem, b), {"cls": 1 - core})

    def inv_wait(b):
        arrived(inv.at[b, 1 - core], at(ic_sem, b))

    def solve(b):
        piece = total(b)
        inv_wait(b)
        half = width // 2
        for c in range(2):
            out = lax.dot_general(
                piece, inv[b, c].reshape(half, width),
                (((1,), (1,)), ((), ())), preferred_element_type=F32,
            )
            chg[b, me, :, c * half : (c + 1) * half] = out.astype(BF16)
        gather_first(chg.at[b], cz_sem, cy_sem, b)

    def update(b):
        gather_third(chg.at[b], cy_sem, b)
        save = pltpu.make_async_copy(chg.at[b], changes_ref.at[b], out_sem.at[b])
        save.start()
        change = chg[b].reshape(classes, width)
        high = tile_of(rows, 256)

        @pl.loop(0, rows // high)
        def _(t):
            here = pl.ds(pl.multiple_of(t * high, high), high)
            resid[here, :] = resid[here, :] - lax.dot_general(
                feats[here, b * width : (b + 1) * width], change,
                (((1,), (1,)), ((), ())), preferred_element_type=F32,
            )

        return save

    correlate(0)
    for d in range(1, n):
        arrived(abuf.at[lax.rem(me - d + n, n)], at(a_sem, d))
    own.wait()
    for b in range(blocks):
        inv[b, core, me] = abuf[roots_ref[b]]
    inv_first(0)
    scatter(0)
    inv_second(0)
    saves = []
    for b in range(blocks):
        if b + 1 < blocks:
            inv_first(b + 1)
        if b == 0:
            inv_third(0)
        solve(b)
        if b + 1 < blocks:
            inv_second(b + 1)
        gather_second(chg.at[b], cz_sem, cy_sem, b)
        saves.append(update(b))
        if b + 1 < blocks:
            correlate(b + 1)
            inv_third(b + 1)
            scatter(b + 1)
    res_ref[...] = resid[...].astype(BF16)
    for save in saves:
        save.wait()
    for copy in pending:
        copy.wait_send()


def per_device(n, embeddings, omega, phases, index_list, inverse_store, roots, residual_in):
    rows, din = embeddings.shape
    pool = omega.shape[1]
    width = inverse_store.shape[1]
    blocks = roots.shape[0]
    classes = residual_in.shape[1]
    inner = 2
    outer = n // inner
    share = classes // n
    part = width // (2 * n)
    vmem = pl.BlockSpec(memory_space=pltpu.VMEM)
    anywhere = pl.BlockSpec(memory_space=pl.ANY)
    dma = pltpu.SemaphoreType.DMA
    flops = 2 * rows * pool * (din + pool + 2 * classes)
    changes, residual = pl.pallas_call(
        functools.partial(body, n, inner),
        out_shape=(
            jax.ShapeDtypeStruct((blocks, n, share, width), BF16),
            jax.ShapeDtypeStruct((rows, classes), BF16),
        ),
        in_specs=[pl.BlockSpec(memory_space=pltpu.SMEM), vmem, vmem, vmem, vmem, anywhere, anywhere],
        out_specs=(anywhere, vmem),
        scratch_shapes=[
            pltpu.VMEM((rows, pool), BF16),
            pltpu.VMEM((rows, pool), BF16),
            pltpu.VMEM((rows, classes), F32),
            pltpu.VMEM((blocks, n, share, width), BF16),
            pltpu.VMEM((blocks, outer, share, width), BF16),
            pltpu.VMEM((blocks, outer, share, width), BF16),
            pltpu.VMEM((blocks, outer, share, width), BF16),
            pltpu.VMEM((blocks, n, share, width), BF16),
            pltpu.VMEM((n, part, width), BF16),
            pltpu.VMEM((blocks, 2, n, part, width), BF16),
            dma((2, n)),
            dma((2, blocks, outer)),
            dma((2, blocks, outer)),
            dma((2, blocks, outer)),
            dma((2, blocks, outer)),
            dma((2, blocks, outer)),
            dma((2, blocks, outer)),
            dma((2, blocks)),
            dma((2,)),
            dma((blocks,)),
        ],
        compiler_params=pltpu.CompilerParams(
            collective_id=0, has_side_effects=True, vmem_limit_bytes=56 * 1024 * 1024
        ),
        cost_estimate=pl.CostEstimate(
            flops=flops, bytes_accessed=20 * 1024 * 1024, transcendentals=rows * pool
        ),
    )(
        roots, embeddings, omega, phases[None, :], index_list[None, :],
        inverse_store[0].reshape(2, n, part, width), residual_in,
    )
    changes = jnp.swapaxes(changes.reshape(blocks, classes, width), 1, 2)
    return changes, residual


def solution(mesh):
    in_specs = (
        P(("groups", "rows"), None),
        P(),
        P(),
        P(),
        P(("groups", "rows"), None, None),
        P(),
        P(("groups", "rows"), "cls"),
    )
    out_specs = (P("groups", None, "cls"), P(("groups", "rows"), "cls"))
    return jax.shard_map(
        functools.partial(per_device, mesh.shape["rows"]),
        mesh=mesh, in_specs=in_specs, out_specs=out_specs, check_vma=False,
    )
```

```python
import functools
import math

import jax
import jax.numpy as jnp
import numpy as np
from jax import lax
from jax.experimental import pallas as pl
from jax.experimental.pallas import tpu as pltpu
from jax.sharding import PartitionSpec as P

MESH = pl.DeviceIdType.MESH
F32 = jnp.float32
BF16 = jnp.bfloat16


def cos_coefficients(degree):
    top = math.pi**2 * 1.0001
    cheb = np.polynomial.chebyshev.Chebyshev.interpolate(
        lambda u: np.cos(np.sqrt(np.maximum(u, 0.0))), degree, domain=[0.0, top]
    )
    return [float(c) for c in cheb.convert(kind=np.polynomial.Polynomial).coef]


COS = cos_coefficients(7)
TWO_PI_HI = 6.28125
TWO_PI_LO = 2.0 * math.pi - TWO_PI_HI


def cosine(x):
    turns = jnp.round(x * (1.0 / (2.0 * math.pi)))
    r = (x - turns * TWO_PI_HI) - turns * TWO_PI_LO
    u = r * r
    y = jnp.full_like(u, COS[-1])
    for c in COS[-2::-1]:
        y = y * u + c
    return y


def tile_of(size, want):
    return want if size % want == 0 else size


def body(
    n, inner, blocks, halves, roots_ref, emb_ref, omega_ref, phases_ref, index_ref, slot_ref, res_in_ref,
    changes_ref, res_ref,
    plain, feats, resid, corr, ybuf, zout, zbuf, pair, chg, abuf, inv,
    a_sem, ys_sem, zs_sem, p_sem, cz_sem, cy_sem, iz_sem, ic_sem, loc_sem, out_sem,
):
    outer = n // inner
    me = lax.axis_index("rows")
    core = lax.axis_index("cls")
    mi = lax.rem(me, inner)
    mo = lax.div(me, inner)
    partner = mo * inner + (inner - 1 - mi)
    rows, din = emb_ref.shape
    pool = omega_ref.shape[1]
    width = corr.shape[3]
    lines = resid.shape[1] // halves
    share = lines // n
    fold = width // inner
    pending = []

    def send(src, dst, sems, device):
        copy = pltpu.make_async_remote_copy(
            src_ref=src, dst_ref=dst, send_sem=sems[0], recv_sem=sems[1],
            device_id=device, device_id_type=MESH,
        )
        copy.start()
        pending.append(copy)
        return copy

    def arrived(dst, sems):
        pltpu.make_async_remote_copy(
            src_ref=dst, dst_ref=dst, send_sem=sems[0], recv_sem=sems[1],
            device_id={"rows": partner}, device_id_type=MESH,
        ).wait_recv()

    def at(sem, *idx):
        return sem.at[(0, *idx)], sem.at[(1, *idx)]

    def other(d):
        return lax.rem(mo + d, outer)

    barrier = pltpu.get_barrier_semaphore()
    for d in range(1, n):
        pl.semaphore_signal(
            barrier, inc=1, device_id={"rows": lax.rem(me + d, n)}, device_id_type=MESH
        )
    pl.semaphore_signal(barrier, inc=1, device_id={"cls": 1 - core}, device_id_type=MESH)
    pl.semaphore_wait(barrier, n)

    for d in range(1, n):
        to = lax.rem(me + d, n)
        send(
            slot_ref.at[lax.rem(to, inner), core, lax.div(to, inner)], abuf.at[me],
            at(a_sem, d), {"rows": to},
        )
    own = pltpu.make_async_copy(slot_ref.at[mi, core, mo], abuf.at[me], loc_sem.at[0])
    own.start()
    res_load = pltpu.make_async_copy(res_in_ref, res_ref, loc_sem.at[1])
    res_load.start()

    scale = math.sqrt(2.0 / width)
    wide = tile_of(pool, 512)

    @pl.loop(0, pool // wide)
    def _(t):
        cols = pl.ds(pl.multiple_of(t * wide, wide), wide)
        proj = jnp.dot(emb_ref[...], omega_ref[:, cols], preferred_element_type=F32)
        plain[:, cols] = (scale * cosine(proj + phases_ref[:, cols])).astype(BF16)

    narrow = tile_of(pool, 256)

    @pl.loop(0, pool // narrow)
    def _(t):
        cols = pl.ds(pl.multiple_of(t * narrow, narrow), narrow)
        line = lax.broadcasted_iota(jnp.int32, (pool, narrow), 0)
        pick = jnp.where(line == index_ref[:, cols], 1.0, 0.0).astype(BF16)
        feats[:, cols] = jnp.dot(plain[...], pick, preferred_element_type=F32).astype(BF16)

    res_load.wait()
    resid[...] = res_ref[...].astype(F32)

    step = tile_of(width, 256)

    def correlate(b, h):
        k = b * halves + h
        rounded = resid[:, h * lines : (h + 1) * lines].astype(BF16)

        @pl.loop(0, width // step)
        def _(t):
            here = pl.multiple_of(t * step, step)
            part = lax.dot_general(
                rounded, feats[:, pl.ds(b * width + here, step)],
                (((0,), (0,)), ((), ())), preferred_element_type=F32,
            )
            corr[k, :, :, pl.ds(here, step)] = part.astype(BF16).reshape(n, share, step)

        for d in range(1, outer + 1):
            o = other(d)
            send(
                corr.at[k, o * inner + (inner - 1 - mi)], ybuf.at[k, o],
                at(ys_sem, k, d % outer), {"rows": partner},
            )

    def pair_sum(k, d):
        o = other(d)
        arrived(ybuf.at[k, o], at(ys_sem, k, d % outer))
        return corr[k, o * inner + mi].astype(F32) + ybuf[k, o].astype(F32)

    def scatter(k):
        for d in range(1, outer):
            o = other(d)
            zout[k, d] = pair_sum(k, d).astype(BF16)
            send(zout.at[k, d], zbuf.at[k, d], at(zs_sem, k, d), {"rows": o * inner + mi})

    def total(k):
        acc = pair_sum(k, 0)
        for d in range(1, outer):
            arrived(zbuf.at[k, d], at(zs_sem, k, d))
            acc = acc + zbuf[k, d].astype(F32)
        pair[k, mi] = acc.astype(BF16)
        send(pair.at[k, mi], pair.at[k, mi], at(p_sem, k), {"rows": partner})

    def inv_spread(b):
        for d in range(1, outer):
            send(
                inv.at[b, core, mo], inv.at[b, core, mo], at(iz_sem, b, d),
                {"rows": other(d) * inner + mi},
            )

    def inv_share(b):
        for d in range(1, outer):
            arrived(inv.at[b, core, lax.rem(mo - d + outer, outer)], at(iz_sem, b, d))
        send(inv.at[b, core], inv.at[b, core], at(ic_sem, b), {"cls": 1 - core})

    def inv_wait(b):
        arrived(inv.at[b, 1 - core], at(ic_sem, b))

    def solve(b, h):
        k = b * halves + h
        arrived(pair.at[k, inner - 1 - mi], at(p_sem, k))
        both = pair[k].reshape(inner * share, width)
        out = lax.dot_general(
            both, inv[b].reshape(fold, width),
            (((1,), (1,)), ((), ())), preferred_element_type=F32,
        )
        chg[k, mi, mo] = out.astype(BF16)
        mine = chg.at[k, mi, mo]
        for d in range(1, outer):
            send(mine, mine, at(cz_sem, k, d), {"rows": other(d) * inner + mi})
        send(mine, mine, at(cy_sem, k, 0), {"rows": partner})

    def forward(k):
        for d in range(1, outer):
            block = chg.at[k, mi, lax.rem(mo - d + outer, outer)]
            arrived(block, at(cz_sem, k, d))
            send(block, block, at(cy_sem, k, d), {"rows": partner})

    saves = []

    def update(b, h):
        k = b * halves + h
        for d in range(outer):
            arrived(chg.at[k, inner - 1 - mi, lax.rem(mo - d + outer, outer)], at(cy_sem, k, d))
        save = pltpu.make_async_copy(chg.at[k], changes_ref.at[k], out_sem.at[k])
        save.start()
        saves.append(save)
        high = tile_of(rows, 256)

        @pl.loop(0, rows // high)
        def _(t):
            here = pl.ds(pl.multiple_of(t * high, high), high)
            there = slice(h * lines, (h + 1) * lines)
            drop = jnp.zeros((high, lines), F32)
            for i in range(inner):
                first = b * width + i * fold
                drop = drop + lax.dot_general(
                    feats[here, first : first + fold], chg[k, i].reshape(lines, fold),
                    (((1,), (1,)), ((), ())), preferred_element_type=F32,
                )
            resid[here, there] = resid[here, there] - drop

    every = range(halves)
    for h in every:
        correlate(0, h)
    for d in range(1, n):
        arrived(abuf.at[lax.rem(me - d + n, n)], at(a_sem, d))
    own.wait()
    for b in range(blocks):
        inv[b, core, mo] = abuf[roots_ref[b]]
    inv_spread(0)
    for b in range(blocks):
        more = b + 1 < blocks
        for h in every:
            scatter(b * halves + h)
        if b == 0:
            inv_share(0)
        for h in every:
            total(b * halves + h)
        inv_wait(b)
        for h in every:
            solve(b, h)
        if more:
            inv_spread(b + 1)
        for h in every:
            forward(b * halves + h)
        for h in every:
            update(b, h)
            if more:
                correlate(b + 1, h)
                if h == 0:
                    inv_share(b + 1)
    res_ref[...] = resid[...].astype(BF16)
    for save in saves:
        save.wait()
    for copy in pending:
        copy.wait_send()


def per_device(n, embeddings, omega, phases, index_list, inverse_store, roots, residual_in):
    rows, din = embeddings.shape
    pool = omega.shape[1]
    width = inverse_store.shape[1]
    blocks = roots.shape[0]
    classes = residual_in.shape[1]
    inner = 2
    outer = n // inner
    halves = 2 if classes % (2 * n * 16) == 0 else 1
    count = blocks * halves
    lines = classes // halves
    share = lines // n
    part = width // (2 * n)
    fold = width // inner
    vmem = pl.BlockSpec(memory_space=pltpu.VMEM)
    anywhere = pl.BlockSpec(memory_space=pl.ANY)
    dma = pltpu.SemaphoreType.DMA
    flops = 2 * rows * pool * (din + pool + 2 * classes)
    changes, residual = pl.pallas_call(
        functools.partial(body, n, inner, blocks, halves),
        out_shape=(
            jax.ShapeDtypeStruct((count, inner, outer, inner * share, fold), BF16),
            jax.ShapeDtypeStruct((rows, classes), BF16),
        ),
        in_specs=[pl.BlockSpec(memory_space=pltpu.SMEM), vmem, vmem, vmem, vmem, anywhere, anywhere],
        out_specs=(anywhere, vmem),
        scratch_shapes=[
            pltpu.VMEM((rows, pool), BF16),
            pltpu.VMEM((rows, pool), BF16),
            pltpu.VMEM((rows, classes), F32),
            pltpu.VMEM((count, n, share, width), BF16),
            pltpu.VMEM((count, outer, share, width), BF16),
            pltpu.VMEM((count, outer, share, width), BF16),
            pltpu.VMEM((count, outer, share, width), BF16),
            pltpu.VMEM((count, inner, share, width), BF16),
            pltpu.VMEM((count, inner, outer, inner * share, fold), BF16),
            pltpu.VMEM((n, part, width), BF16),
            pltpu.VMEM((blocks, 2, outer, part, width), BF16),
            dma((2, n)),
            dma((2, count, outer)),
            dma((2, count, outer)),
            dma((2, count)),
            dma((2, count, outer)),
            dma((2, count, outer)),
            dma((2, blocks, outer)),
            dma((2, blocks)),
            dma((2,)),
            dma((count,)),
        ],
        compiler_params=pltpu.CompilerParams(
            collective_id=0, has_side_effects=True, vmem_limit_bytes=56 * 1024 * 1024
        ),
        cost_estimate=pl.CostEstimate(
            flops=flops, bytes_accessed=20 * 1024 * 1024, transcendentals=rows * pool
        ),
    )(
        roots, embeddings, omega, phases[None, :], index_list[None, :],
        inverse_store[0].reshape(inner, 2, outer, part, width), residual_in,
    )
    changes = changes.reshape(blocks, halves, inner, lines, fold).transpose(0, 2, 4, 1, 3)
    changes = changes.reshape(blocks, width, classes)
    return changes, residual


def solution(mesh):
    in_specs = (
        P(("groups", "rows"), None),
        P(),
        P(),
        P(),
        P(("groups", "rows"), None, None),
        P(),
        P(("groups", "rows"), "cls"),
    )
    out_specs = (P("groups", None, "cls"), P(("groups", "rows"), "cls"))
    return jax.shard_map(
        functools.partial(per_device, mesh.shape["rows"]),
        mesh=mesh, in_specs=in_specs, out_specs=out_specs, check_vma=False,
    )
```

```python
import functools
import math

import jax
import jax.numpy as jnp
import numpy as np
from jax import lax
from jax.experimental import pallas as pl
from jax.experimental.pallas import tpu as pltpu
from jax.sharding import PartitionSpec as P

MESH = pl.DeviceIdType.MESH
F32 = jnp.float32
BF16 = jnp.bfloat16


def cos_coefficients(degree):
    top = math.pi**2 * 1.0001
    cheb = np.polynomial.chebyshev.Chebyshev.interpolate(
        lambda u: np.cos(np.sqrt(np.maximum(u, 0.0))), degree, domain=[0.0, top]
    )
    return [float(c) for c in cheb.convert(kind=np.polynomial.Polynomial).coef]


COS = cos_coefficients(7)
TWO_PI_HI = 6.28125
TWO_PI_LO = 2.0 * math.pi - TWO_PI_HI


def cosine(x):
    turns = jnp.round(x * (1.0 / (2.0 * math.pi)))
    r = (x - turns * TWO_PI_HI) - turns * TWO_PI_LO
    u = r * r
    y = jnp.full_like(u, COS[-1])
    for c in COS[-2::-1]:
        y = y * u + c
    return y


def tile_of(size, want):
    return want if size % want == 0 else size


def body(
    n, inner, blocks, halves, roots_ref, emb_ref, omega_ref, phases_ref, index_ref, slot_ref, res_in_ref,
    changes_ref, res_ref,
    plain, feats, resid, corr, ybuf, zout, zbuf, pair, chg, abuf, inv,
    a_sem, ys_sem, zs_sem, p_sem, cz_sem, cy_sem, iz_sem, ic_sem, loc_sem, out_sem,
):
    outer = n // inner
    me = lax.axis_index("rows")
    core = lax.axis_index("cls")
    mi = lax.rem(me, inner)
    mo = lax.div(me, inner)
    partner = mo * inner + (inner - 1 - mi)
    rows, din = emb_ref.shape
    pool = omega_ref.shape[1]
    width = corr.shape[3]
    lines = resid.shape[1] // halves
    share = lines // n
    fold = width // inner
    pending = []

    def send(src, dst, sems, device):
        copy = pltpu.make_async_remote_copy(
            src_ref=src, dst_ref=dst, send_sem=sems[0], recv_sem=sems[1],
            device_id=device, device_id_type=MESH,
        )
        copy.start()
        pending.append(copy)
        return copy

    def arrived(dst, sems):
        pltpu.make_async_remote_copy(
            src_ref=dst, dst_ref=dst, send_sem=sems[0], recv_sem=sems[1],
            device_id={"rows": partner}, device_id_type=MESH,
        ).wait_recv()

    def at(sem, *idx):
        return sem.at[(0, *idx)], sem.at[(1, *idx)]

    def other(d):
        return lax.rem(mo + d, outer)

    barrier = pltpu.get_barrier_semaphore()
    for d in range(1, n):
        pl.semaphore_signal(
            barrier, inc=1, device_id={"rows": lax.rem(me + d, n)}, device_id_type=MESH
        )
    pl.semaphore_signal(barrier, inc=1, device_id={"cls": 1 - core}, device_id_type=MESH)
    pl.semaphore_wait(barrier, n)

    for d in range(1, n):
        to = lax.rem(me + d, n)
        send(
            slot_ref.at[lax.rem(to, inner), core, lax.div(to, inner)], abuf.at[me],
            at(a_sem, d), {"rows": to},
        )
    own = pltpu.make_async_copy(slot_ref.at[mi, core, mo], abuf.at[me], loc_sem.at[0])
    own.start()
    res_load = pltpu.make_async_copy(res_in_ref, res_ref, loc_sem.at[1])
    res_load.start()

    scale = math.sqrt(2.0 / width)
    wide = tile_of(pool, 512)

    @pl.loop(0, pool // wide)
    def _(t):
        cols = pl.ds(pl.multiple_of(t * wide, wide), wide)
        proj = jnp.dot(emb_ref[...], omega_ref[:, cols], preferred_element_type=F32)
        plain[:, cols] = (scale * cosine(proj + phases_ref[:, cols])).astype(BF16)

    narrow = tile_of(pool, 256)

    @pl.loop(0, pool // narrow)
    def _(t):
        cols = pl.ds(pl.multiple_of(t * narrow, narrow), narrow)
        line = lax.broadcasted_iota(jnp.int32, (pool, narrow), 0)
        pick = jnp.where(line == index_ref[:, cols], 1.0, 0.0).astype(BF16)
        feats[:, cols] = jnp.dot(plain[...], pick, preferred_element_type=F32).astype(BF16)

    res_load.wait()
    resid[...] = res_ref[...].astype(F32)

    step = tile_of(width, 256)

    def correlate(b, h):
        k = b * halves + h
        rounded = resid[:, h * lines : (h + 1) * lines].astype(BF16)

        @pl.loop(0, width // step)
        def _(t):
            here = pl.multiple_of(t * step, step)
            part = lax.dot_general(
                rounded, feats[:, pl.ds(b * width + here, step)],
                (((0,), (0,)), ((), ())), preferred_element_type=F32,
            )
            corr[k, :, :, pl.ds(here, step)] = part.astype(BF16).reshape(n, share, step)

        for d in range(1, outer + 1):
            o = other(d)
            send(
                corr.at[k, o * inner + (inner - 1 - mi)], ybuf.at[k, o],
                at(ys_sem, k, d % outer), {"rows": partner},
            )

    def pair_sum(k, d):
        o = other(d)
        arrived(ybuf.at[k, o], at(ys_sem, k, d % outer))
        return corr[k, o * inner + mi].astype(F32) + ybuf[k, o].astype(F32)

    def scatter(k):
        for d in sorted(range(1, outer), key=lambda d: abs(2 * d - outer)):
            o = other(d)
            zout[k, d] = pair_sum(k, d).astype(BF16)
            send(zout.at[k, d], zbuf.at[k, d], at(zs_sem, k, d), {"rows": o * inner + mi})

    def total(k):
        acc = pair_sum(k, 0)
        for d in sorted(range(1, outer), key=lambda d: abs(2 * d - outer)):
            arrived(zbuf.at[k, d], at(zs_sem, k, d))
            acc = acc + zbuf[k, d].astype(F32)
        pair[k, mi] = acc.astype(BF16)
        send(pair.at[k, mi], pair.at[k, mi], at(p_sem, k), {"rows": partner})

    def inv_spread(b):
        for d in sorted(range(1, outer), key=lambda d: abs(2 * d - outer)):
            send(
                inv.at[b, core, mo], inv.at[b, core, mo], at(iz_sem, b, d),
                {"rows": other(d) * inner + mi},
            )

    def inv_share(b):
        for d in sorted(range(1, outer), key=lambda d: abs(2 * d - outer)):
            arrived(inv.at[b, core, lax.rem(mo - d + outer, outer)], at(iz_sem, b, d))
        send(inv.at[b, core], inv.at[b, core], at(ic_sem, b), {"cls": 1 - core})

    def inv_wait(b):
        arrived(inv.at[b, 1 - core], at(ic_sem, b))

    def solve(b, h):
        k = b * halves + h
        arrived(pair.at[k, inner - 1 - mi], at(p_sem, k))
        both = pair[k].reshape(inner * share, width)
        out = lax.dot_general(
            both, inv[b].reshape(fold, width),
            (((1,), (1,)), ((), ())), preferred_element_type=F32,
        )
        chg[k, mi, mo] = out.astype(BF16)
        mine = chg.at[k, mi, mo]
        for d in sorted(range(1, outer), key=lambda d: abs(2 * d - outer)):
            send(mine, mine, at(cz_sem, k, d), {"rows": other(d) * inner + mi})
        send(mine, mine, at(cy_sem, k, 0), {"rows": partner})

    def forward(k):
        for d in sorted(range(1, outer), key=lambda d: abs(2 * d - outer)):
            block = chg.at[k, mi, lax.rem(mo - d + outer, outer)]
            arrived(block, at(cz_sem, k, d))
            send(block, block, at(cy_sem, k, d), {"rows": partner})

    saves = []

    def update(b, h):
        k = b * halves + h
        for d in range(outer):
            arrived(chg.at[k, inner - 1 - mi, lax.rem(mo - d + outer, outer)], at(cy_sem, k, d))
        save = pltpu.make_async_copy(chg.at[k], changes_ref.at[k], out_sem.at[k])
        save.start()
        saves.append(save)
        high = tile_of(rows, 256)

        @pl.loop(0, rows // high)
        def _(t):
            here = pl.ds(pl.multiple_of(t * high, high), high)
            there = slice(h * lines, (h + 1) * lines)
            drop = jnp.zeros((high, lines), F32)
            for i in range(inner):
                first = b * width + i * fold
                drop = drop + lax.dot_general(
                    feats[here, first : first + fold], chg[k, i].reshape(lines, fold),
                    (((1,), (1,)), ((), ())), preferred_element_type=F32,
                )
            resid[here, there] = resid[here, there] - drop

    every = range(halves)
    for h in every:
        correlate(0, h)
    for d in range(1, n):
        arrived(abuf.at[lax.rem(me - d + n, n)], at(a_sem, d))
    own.wait()
    for b in range(blocks):
        inv[b, core, mo] = abuf[roots_ref[b]]
    inv_spread(0)
    for b in range(blocks):
        more = b + 1 < blocks
        for h in every:
            scatter(b * halves + h)
        if b == 0:
            inv_share(0)
        for h in every:
            total(b * halves + h)
            if h == 0:
                inv_wait(b)
            solve(b, h)
        if more:
            inv_spread(b + 1)
        for h in every:
            forward(b * halves + h)
        for h in every:
            update(b, h)
            if more:
                correlate(b + 1, h)
                if h == 0:
                    inv_share(b + 1)
    res_ref[...] = resid[...].astype(BF16)
    for save in saves:
        save.wait()
    for copy in pending:
        copy.wait_send()


def per_device(n, embeddings, omega, phases, index_list, inverse_store, roots, residual_in):
    rows, din = embeddings.shape
    pool = omega.shape[1]
    width = inverse_store.shape[1]
    blocks = roots.shape[0]
    classes = residual_in.shape[1]
    inner = 2
    outer = n // inner
    halves = 2 if classes % (2 * n * 16) == 0 else 1
    count = blocks * halves
    lines = classes // halves
    share = lines // n
    part = width // (2 * n)
    fold = width // inner
    vmem = pl.BlockSpec(memory_space=pltpu.VMEM)
    anywhere = pl.BlockSpec(memory_space=pl.ANY)
    dma = pltpu.SemaphoreType.DMA
    flops = 2 * rows * pool * (din + pool + 2 * classes)
    changes, residual = pl.pallas_call(
        functools.partial(body, n, inner, blocks, halves),
        out_shape=(
            jax.ShapeDtypeStruct((count, inner, outer, inner * share, fold), BF16),
            jax.ShapeDtypeStruct((rows, classes), BF16),
        ),
        in_specs=[pl.BlockSpec(memory_space=pltpu.SMEM), vmem, vmem, vmem, vmem, anywhere, anywhere],
        out_specs=(anywhere, vmem),
        scratch_shapes=[
            pltpu.VMEM((rows, pool), BF16),
            pltpu.VMEM((rows, pool), BF16),
            pltpu.VMEM((rows, classes), F32),
            pltpu.VMEM((count, n, share, width), BF16),
            pltpu.VMEM((count, outer, share, width), BF16),
            pltpu.VMEM((count, outer, share, width), BF16),
            pltpu.VMEM((count, outer, share, width), BF16),
            pltpu.VMEM((count, inner, share, width), BF16),
            pltpu.VMEM((count, inner, outer, inner * share, fold), BF16),
            pltpu.VMEM((n, part, width), BF16),
            pltpu.VMEM((blocks, 2, outer, part, width), BF16),
            dma((2, n)),
            dma((2, count, outer)),
            dma((2, count, outer)),
            dma((2, count)),
            dma((2, count, outer)),
            dma((2, count, outer)),
            dma((2, blocks, outer)),
            dma((2, blocks)),
            dma((2,)),
            dma((count,)),
        ],
        compiler_params=pltpu.CompilerParams(
            collective_id=0, has_side_effects=True, vmem_limit_bytes=56 * 1024 * 1024
        ),
        cost_estimate=pl.CostEstimate(
            flops=flops, bytes_accessed=20 * 1024 * 1024, transcendentals=rows * pool
        ),
    )(
        roots, embeddings, omega, phases[None, :], index_list[None, :],
        inverse_store[0].reshape(inner, 2, outer, part, width), residual_in,
    )
    changes = changes.reshape(blocks, halves, inner, lines, fold).transpose(0, 2, 4, 1, 3)
    changes = changes.reshape(blocks, width, classes)
    return changes, residual


def solution(mesh):
    in_specs = (
        P(("groups", "rows"), None),
        P(),
        P(),
        P(),
        P(("groups", "rows"), None, None),
        P(),
        P(("groups", "rows"), "cls"),
    )
    out_specs = (P("groups", None, "cls"), P(("groups", "rows"), "cls"))
    return jax.shard_map(
        functools.partial(per_device, mesh.shape["rows"]),
        mesh=mesh, in_specs=in_specs, out_specs=out_specs, check_vma=False,
    )
```
